32 devices in a mesh: groups: 2 (over y), blk: 16 (over z, x, core).
Axes of the slice: x: 2, y: 2, z: 4, core: 2. Of those that a mesh axis runs over, the one named last changes fastest.
Arguments:
- queries: bfloat16 [128, 4096], P(('groups', 'blk')), parts along dimension 0, may hold values from -150 to 150
- k_cache: bfloat16 [32768, 512], P(('groups', 'blk')), parts along dimension 0, may hold values from -6 to 6
- v_cache: bfloat16 [32768, 512], P(('groups', 'blk')), parts along dimension 0, may hold values from -6 to 6
- w_out: bfloat16 [4096, 2048], P('blk'), may hold values from -0.09375 to 0.09375
- residual: bfloat16 [128, 2048], P(('groups', 'blk')), parts along dimension 0, may hold values from -6 to 6
- norm_gain: float32 [2048], replicated, may hold values from 0.1 to 1.9
- expert_ids: int32 [128, 8], P('groups'), parts along dimension 0, may hold values from 0 to 15, all different within a row; in each aligned block of 64 rows (0 to 63, 64 to 127, ...) at most 64 rows name the same one
- gate_fixed: int32 [128, 8], P('groups'), parts along dimension 0, may hold values from 1 to 65535
- w_gate: bfloat16 [16, 2048, 768], P('blk'), may hold values from -0.125 to 0.125
- w_up: bfloat16 [16, 2048, 768], P('blk'), may hold values from -0.125 to 0.125
- w_down: bfloat16 [16, 768, 2048], P('blk'), may hold values from -0.21875 to 0.21875
Outputs:
- hidden: bfloat16 [128, 2048], P(('groups', 'blk')), parts along dimension 0
- moe_out: bfloat16 [128, 2048], P(('groups', 'blk')), parts along dimension 0
The draws below stay inside these ranges and needn't reach their ends.
There are 2 independent parts, one for each index of `groups`. The reference program is written for one: setup_inputs(seed, part) draws one part's arguments, and reference() takes and returns one part's arrays. A program takes and returns all parts, laid end to end along the dimension named above; an argument that names none is the same for every part. Nothing has to cross between parts.
Inputs may be any that keep to these rules, and one draw needn't show every extreme that they name: `expert_ids`: each row names 8 different experts; no expert is named by more than 64 rows of a part, a bound that some block reaches.
All inputs are finite; a program needn't handle non-finite values.
Results may differ from the reference program's by a relative error of at most 0.0075.
Values may be sent and summed in bfloat16 or wider, within the bound.
A program may use at most 128 MiB of HBM per device.

```python
import math
import jax
import jax.numpy as jnp
import numpy as np
from jax import lax

D = 2048
FF = 768
HEADS = 32
KV_HEADS = 4
HEAD_DIM = 128
TOPK = 8
CACHE_DEV = 1024
GROUP = 8
EXPERTS = 16
QUERY_ROWS = 64
CACHE_LEN = 16384
CAPACITY = 64
N_BLK = 16


def cache_keys(key):
    width = KV_HEADS * HEAD_DIM
    base = jax.random.normal(jax.random.fold_in(key, 101), (CACHE_LEN, width), jnp.float32)
    base = jnp.clip(base, -6.0, 6.0)
    return base


def draw_k_cache(key, part):
    return cache_keys(key).astype(jnp.bfloat16)


def draw_queries(key, part):
    width = HEADS * HEAD_DIM
    base = jnp.clip(3.0 * jax.random.normal(jax.random.fold_in(key, 107), (QUERY_ROWS, width), jnp.float32), -18.0, 18.0)
    return base.astype(jnp.bfloat16)


def touch_ends(entries, key, low, top_value):
    dims = entries.shape
    spot = [jax.random.randint(jax.random.fold_in(key, axis), (), 0, dims[axis]) for axis in range(len(dims))]
    entries = entries.at[tuple(spot)].set(low)
    longest = dims.index(max(dims))
    spot[longest] = (spot[longest] + 1) % dims[longest]
    return entries.at[tuple(spot)].set(top_value)


def block_scale(key, extent, pieces, low, top_value):
    def one(axis_at, shards_of):
        heights = jax.random.uniform(jax.random.fold_in(jax.random.fold_in(key, 6), axis_at), (shards_of,), jnp.float32, low / len(pieces), top_value / len(pieces))
        return jnp.repeat(jnp.exp(heights), extent[axis_at] // shards_of).reshape((-1,) + (1,) * (len(extent) - axis_at - 1))

    factor_of = one(*pieces[0])
    for cut in pieces[1:]:
        factor_of = factor_of * one(*cut)
    return factor_of


def shared_out(own_key, own, number, rows, amount, top, bound, slope):
    ranking = jax.random.permutation(own_key, amount)
    heavy_load, common = portions_of(amount, rows * top, bound, slope, True), portions_of(amount, rows * top, bound, slope, False)
    places = jnp.arange(amount)

    def named(tallies, offset_by):
        used = int((tallies > 0).sum())
        fixed = max(1, used // 4)
        moved = fixed + (places - fixed + offset_by * (used - fixed)) % max(1, amount - fixed)
        return jnp.zeros((amount,), jnp.int32).at[ranking[jnp.where(places < fixed, places, moved)]].set(jnp.asarray(tallies, jnp.int32))

    tallies = jnp.where(number % 4 == 0, named(heavy_load, number // 4), named(common, number - number // 4 - 1))
    mixed = jax.random.permutation(jax.random.fold_in(own, 3), amount)
    donor, receiver = mixed[0:amount // 2 * 2:2], mixed[1:amount // 2 * 2:2]
    slack = jnp.minimum(tallies[donor] - 1, bound - tallies[receiver]) // 2
    slack = jnp.where((donor == ranking[0]) | (receiver == ranking[0]) | (tallies[receiver] == 0), 0, jnp.maximum(slack, 0))
    moved = jax.random.randint(jax.random.fold_in(own, 4), (amount // 2,), 0, 1 << 20) % (slack + 1)
    tallies = tallies.at[donor].add(-moved).at[receiver].add(moved)
    members = jnp.searchsorted(jnp.cumsum(tallies), jnp.arange(rows * top), side="right").astype(jnp.int32)
    table = members.reshape(top, rows).T
    table = table[jax.random.permutation(jax.random.fold_in(own, 1), rows)]
    offset_by = jax.random.randint(jax.random.fold_in(own, 2), (rows, 1), 0, top)
    return jnp.take_along_axis(table, (jnp.arange(top)[None, :] + offset_by) % top, axis=1)


def portions_of(number_of, total, bound, skew, full):
    weights = [(1 << 20) // math.isqrt(rank ** skew) + 1 for rank in range(1, number_of + 1)]
    largest = bound if full else min(bound, max(-(-total // number_of), total * weights[0] // sum(weights)))
    least = 1 if total - largest >= number_of - 1 else 0
    counts, rest = [largest] + [least] * (number_of - 1), total - largest - least * (number_of - 1)
    while rest > 0:
        candidates = [i for i in range(1, number_of) if counts[i] < largest] or [i for i in range(1, number_of) if counts[i] < bound]
        mass, left = sum([weights[i] for i in candidates]), rest
        for i in candidates:
            extra = min(bound - counts[i], max(1, left * weights[i] // mass), rest)
            counts[i] = counts[i] + extra
            rest = rest - extra
    return np.array(counts)


def bell_draw(key, extent, scale, limit, shards=(), kind=jnp.bfloat16):
    entries = jax.random.normal(key, extent, jnp.float32) * scale
    if len(shards) > 0:
        entries = block_scale(key, extent, shards, -0.22, 0.18) * entries
    return jnp.clip(entries, min=-limit, max=limit).astype(kind)


def setup_inputs(seed: int = 0, part: int = 0) -> dict:
    key_of = jax.random.split(jax.random.key(seed), 12)
    part_keys = jax.random.split(jax.random.fold_in(key_of[11], part), 12)
    queries = draw_queries(jax.random.fold_in(jax.random.fold_in(key_of[11], part), 71), part)
    k_cache = draw_k_cache(jax.random.fold_in(jax.random.fold_in(key_of[11], part), 71), part)
    v_cache = bell_draw(part_keys[2], (CACHE_LEN, KV_HEADS * HEAD_DIM), 1.0, 6.0, ((0, 16),))
    w_out = bell_draw(key_of[3], (HEADS * HEAD_DIM, D), (HEADS * HEAD_DIM) ** -0.5, 0.09375, ((0, 16),))
    residual = bell_draw(part_keys[4], (QUERY_ROWS, D), 1.0, 6.0, ((0, 16),))
    norm_gain = jnp.clip(1.0 + 0.18 * jax.random.normal(key_of[5], (D,), jnp.float32), 0.1, 1.9)
    expert_ids_keys = jax.random.split(jax.random.fold_in(part_keys[6], 1), QUERY_ROWS // QUERY_ROWS)
    expert_ids_turns = jax.random.permutation(jax.random.fold_in(part_keys[6], 3), QUERY_ROWS // QUERY_ROWS)
    expert_ids = jax.vmap(lambda own, number: shared_out(jax.random.fold_in(part_keys[6], 2), own, number, QUERY_ROWS, EXPERTS, TOPK, CAPACITY, 2))(expert_ids_keys, expert_ids_turns).reshape((QUERY_ROWS, TOPK))
    gate_fixed = touch_ends(jax.random.randint(part_keys[7], (QUERY_ROWS, TOPK), 1, 65536), jax.random.fold_in(part_keys[7], 1), 1, 65535).astype(jnp.int32)
    w_gate = bell_draw(key_of[8], (EXPERTS, D, FF), D ** -0.5, 0.125, ((0, 16),))
    w_up = bell_draw(key_of[9], (EXPERTS, D, FF), D ** -0.5, 0.125, ((0, 16),))
    w_down = bell_draw(key_of[10], (EXPERTS, FF, D), FF ** -0.5, 0.21875, ((0, 16),))
    return dict(queries=queries, k_cache=k_cache, v_cache=v_cache, w_out=w_out, residual=residual, norm_gain=norm_gain, expert_ids=expert_ids, gate_fixed=gate_fixed, w_gate=w_gate, w_up=w_up, w_down=w_down)


def merge_state(out_a, max_a, sum_a, out_b, max_b, sum_b):
    top = jnp.maximum(max_a, max_b)
    fac_a = jnp.exp(max_a - top)
    fac_b = jnp.exp(max_b - top)
    return (out_a * fac_a[..., None] + out_b * fac_b[..., None], top, sum_a * fac_a + sum_b * fac_b)

def block_attend(query_four, key_block, value_block):
    span = key_block.shape[0]
    key_three = key_block.astype(jnp.float32).reshape(span, KV_HEADS, HEAD_DIM)
    value_three = value_block.astype(jnp.float32).reshape(span, KV_HEADS, HEAD_DIM)
    scores = jnp.einsum('rhgd,chd->rhgc', query_four, key_three) / jnp.sqrt(jnp.float32(HEAD_DIM))
    block_max = lax.optimization_barrier(jnp.max(scores, axis=-1))
    probs = jnp.exp(scores - block_max[..., None])
    block_sum = lax.optimization_barrier(jnp.sum(probs, axis=-1))
    weights = probs.astype(jnp.bfloat16).astype(jnp.float32)
    block_out = jnp.einsum('rhgc,chd->rhgd', weights, value_three)
    row_count = query_four.shape[0]
    return (block_out.reshape(row_count, HEADS, HEAD_DIM), block_max.reshape(row_count, HEADS), block_sum.reshape(row_count, HEADS))

def reference(queries, k_cache, v_cache, w_out, residual, norm_gain, expert_ids, gate_fixed, w_gate, w_up, w_down):
    row_count = queries.shape[0]
    query_four = queries.astype(jnp.float32).reshape(row_count, KV_HEADS, GROUP, HEAD_DIM)
    key_blocks = k_cache.reshape(N_BLK, CACHE_DEV, KV_HEADS * HEAD_DIM)
    value_blocks = v_cache.reshape(N_BLK, CACHE_DEV, KV_HEADS * HEAD_DIM)

    def visit(carry, pair):
        block = block_attend(query_four, pair[0], pair[1])
        return (merge_state(carry[0], carry[1], carry[2], block[0], block[1], block[2]), None)
    start_state = (jnp.zeros((row_count, HEADS, HEAD_DIM), jnp.float32), jnp.full((row_count, HEADS), -1e+30, jnp.float32), jnp.zeros((row_count, HEADS), jnp.float32))
    state, _ = lax.scan(visit, start_state, (key_blocks, value_blocks))
    attended = (state[0] / state[2][..., None]).reshape(row_count, HEADS * HEAD_DIM).astype(jnp.bfloat16)
    proj = jnp.dot(attended, w_out, preferred_element_type=jnp.float32)
    stream = residual.astype(jnp.float32) + proj
    hidden = stream.astype(jnp.bfloat16)
    normed = (stream * lax.rsqrt(lax.optimization_barrier(jnp.mean(stream * stream, axis=-1, keepdims=True)) + 1e-06) * norm_gain.astype(jnp.float32)).astype(jnp.bfloat16)
    gate_weight = gate_fixed.astype(jnp.float32) / 65536.0
    slot_ids = jnp.arange(CAPACITY, dtype=jnp.int32)

    def one_expert(total, inputs):
        expert, gate_mat, up_mat, down_mat = inputs
        named = expert_ids == expert
        taken = jnp.any(named, axis=1)
        row_weight = lax.optimization_barrier(jnp.sum(jnp.where(named, gate_weight, 0.0), axis=1))
        slot_of = jnp.cumsum(taken.astype(jnp.int32)) - 1
        select = jnp.logical_and(slot_of[None, :] == slot_ids[:, None], taken[None, :])
        picked = jnp.dot(select.astype(jnp.bfloat16), normed, preferred_element_type=jnp.float32).astype(jnp.bfloat16)
        slot_weight = jnp.dot(select.astype(jnp.float32), row_weight, precision=lax.Precision.HIGHEST)
        gate_part = jnp.dot(picked, gate_mat, preferred_element_type=jnp.float32)
        up_part = jnp.dot(picked, up_mat, preferred_element_type=jnp.float32)
        inner = (jax.nn.silu(gate_part) * up_part).astype(jnp.bfloat16)
        result = jnp.dot(inner, down_mat, preferred_element_type=jnp.float32) * slot_weight[:, None]
        back = jnp.dot(select.astype(jnp.float32).T, result, precision=lax.Precision.HIGHEST)
        return (total + back, None)
    total, _ = lax.scan(one_expert, jnp.zeros((row_count, D), jnp.float32), (jnp.arange(EXPERTS, dtype=jnp.int32), w_gate, w_up, w_down))
    return (hidden, total.astype(jnp.bfloat16))
```

```python
import functools
import math

import jax
import jax.numpy as jnp
from jax import lax
from jax.experimental import pallas as pl
from jax.experimental.pallas import tpu as pltpu
from jax.sharding import PartitionSpec as P

HEADS = 32
KV_HEADS = 4
HEAD_DIM = 128
GROUP = 8
CAPACITY = 64


def local_attend(query_rows, k_cache, v_cache):
    row_count = query_rows.shape[0]
    span = k_cache.shape[0]
    query_four = query_rows.reshape(row_count, KV_HEADS, GROUP, HEAD_DIM)
    key_three = k_cache.reshape(span, KV_HEADS, HEAD_DIM)
    value_three = v_cache.reshape(span, KV_HEADS, HEAD_DIM)
    scores = jnp.einsum(
        "rhgd,chd->rhgc", query_four, key_three, preferred_element_type=jnp.float32
    ) / jnp.sqrt(jnp.float32(HEAD_DIM))
    block_max = jnp.max(scores, axis=-1)
    probs = jnp.exp(scores - block_max[..., None])
    block_sum = jnp.sum(probs, axis=-1)
    block_out = jnp.einsum(
        "rhgc,chd->rhgd",
        probs.astype(jnp.bfloat16),
        value_three,
        preferred_element_type=jnp.float32,
    )
    return (
        block_out.reshape(row_count, HEADS * HEAD_DIM),
        block_max.reshape(row_count, HEADS),
        block_sum.reshape(row_count, HEADS),
    )


def shards(
    queries,
    k_cache,
    v_cache,
    w_out,
    residual,
    norm_gain,
    expert_ids,
    gate_fixed,
    w_gate,
    w_up,
    w_down,
):
    row_count = queries.shape[0]
    width_q = HEADS * HEAD_DIM
    devices = lax.axis_size("blk")
    every_query = lax.all_gather(queries, "blk", axis=0, tiled=True)
    total_rows = every_query.shape[0]
    block_rows = 128 if total_rows % 128 == 0 else total_rows
    stacked = every_query.reshape(total_rows // block_rows, block_rows, width_q)
    part_out, part_max, part_sum = lax.map(
        lambda piece: local_attend(piece, k_cache, v_cache), stacked
    )
    part_out = part_out.reshape(total_rows, width_q)
    part_max = part_max.reshape(total_rows, HEADS)
    part_sum = part_sum.reshape(total_rows, HEADS)
    got_out, got_max, got_sum = (
        lax.all_to_all(part_out, "blk", split_axis=0, concat_axis=0, tiled=True),
        lax.all_to_all(part_max, "blk", split_axis=0, concat_axis=0, tiled=True),
        lax.all_to_all(part_sum, "blk", split_axis=0, concat_axis=0, tiled=True),
    )
    got_out = got_out.reshape(devices, row_count, HEADS, HEAD_DIM)
    got_max = got_max.reshape(devices, row_count, HEADS)
    got_sum = got_sum.reshape(devices, row_count, HEADS)
    top = jnp.max(got_max, axis=0)
    factor = jnp.exp(got_max - top[None])
    sum_acc = jnp.sum(got_sum * factor, axis=0)
    out_acc = jnp.sum(got_out * factor[..., None], axis=0).reshape(row_count, width_q)
    attended = (
        (out_acc.reshape(row_count, HEADS, HEAD_DIM) / sum_acc[..., None])
        .reshape(row_count, width_q)
        .astype(jnp.bfloat16)
    )
    columns = lax.all_to_all(attended, "blk", split_axis=1, concat_axis=0, tiled=True)
    piece = columns
    proj = lax.psum_scatter(
        jnp.dot(piece, w_out, preferred_element_type=jnp.float32),
        "blk",
        scatter_dimension=0,
        tiled=True,
    )
    stream = residual.astype(jnp.float32) + proj
    hidden = stream.astype(jnp.bfloat16)
    normed = (
        stream * lax.rsqrt(jnp.mean(stream * stream, axis=-1, keepdims=True) + 1e-06) * norm_gain
    ).astype(jnp.bfloat16)
    every_row = lax.all_gather(normed, "blk", axis=0, tiled=True)
    expert = lax.axis_index("blk")
    named = expert_ids == expert
    taken = jnp.any(named, axis=1)
    row_weight = jnp.sum(jnp.where(named, gate_fixed.astype(jnp.float32) / 65536.0, 0.0), axis=1)
    order = jnp.arange(taken.shape[0], dtype=jnp.int32)
    upto = jnp.logical_and(order[None, :] <= order[:, None], taken[None, :])
    slot_of = jnp.sum(upto.astype(jnp.int32), axis=1) - 1
    slot_ids = jnp.arange(CAPACITY, dtype=jnp.int32)
    select = jnp.logical_and(slot_of[None, :] == slot_ids[:, None], taken[None, :])
    picked = jnp.dot(
        select.astype(jnp.bfloat16), every_row, preferred_element_type=jnp.float32
    ).astype(jnp.bfloat16)
    slot_weight = jnp.dot(select.astype(jnp.float32), row_weight, precision=lax.Precision.HIGHEST)
    gate_part = jnp.dot(picked, w_gate[0], preferred_element_type=jnp.float32)
    up_part = jnp.dot(picked, w_up[0], preferred_element_type=jnp.float32)
    inner = (jax.nn.silu(gate_part) * up_part).astype(jnp.bfloat16)
    result = jnp.dot(inner, w_down[0], preferred_element_type=jnp.float32) * slot_weight[:, None]
    select_back = select.astype(jnp.float32).T
    piece = select_back
    moe_total = lax.psum_scatter(
        jnp.dot(piece, result, precision=lax.Precision.HIGHEST),
        "blk",
        scatter_dimension=0,
        tiled=True,
    )
    return (hidden, moe_total.astype(jnp.bfloat16))


MESH = pl.DeviceIdType.MESH
TILE = 16
F32, BF16 = jnp.float32, jnp.bfloat16


def fits_fused(n, queries, k_cache, v_cache, w_out, residual, gain, ids, gates, w_gate, w_up, w_down):
    rows, width = queries.shape
    heads = width // HEAD_DIM
    return (
        heads % n == 0
        and w_out.shape[0] % HEAD_DIM == 0
        and GROUP % (heads // n) == 0
        and (heads // n) * n * rows == HEAD_DIM
        and w_gate.shape[0] == 1
        and TILE % rows == 0
        and n * TILE == 256
        and residual.shape[1] % (TILE // rows * 128) == 0
    )


def select(out_rows, in_rows, source):
    o = lax.broadcasted_iota(jnp.int32, (out_rows, in_rows), 0)
    i = lax.broadcasted_iota(jnp.int32, (out_rows, in_rows), 1)
    return jnp.where(i == source(o), 1.0, 0.0).astype(BF16)


def dot(a, b, ca=1, cb=0):
    return lax.dot_general(a, b, (((ca,), (cb,)), ((), ())), preferred_element_type=F32)


def fused_kernel(
    n, q_ref, res_ref, gain_ref, ids_ref, gates_ref, k_hbm, v_hbm, wo_hbm, wg_hbm, wu_hbm, wd_hbm,
    hid_ref, moe_ref,
    k_buf, v_buf, wo_buf, wg_buf, wu_buf, wd_buf, q_tmp, t_tmp, s_tmp,
    q_all, o_send, o_got, s_send, s_got, p_send, p_got, n_all, y_send, y_got,
    load_sem, q_ss, q_rs, o_ss, o_rs, s_ss, s_rs, p_ss, p_rs, n_ss, n_rs, y_ss, y_rs,
):
    me = lax.axis_index("blk")
    rows, width = q_ref.shape
    model = res_ref.shape[1]
    heads = width // HEAD_DIM
    kv = heads // GROUP
    own_heads = heads // n
    per_kv = GROUP // own_heads
    total = n * rows
    parts = TILE // rows
    cols = model // parts
    div, rem = lax.div, lax.rem
    scale = math.log2(math.e) / math.sqrt(HEAD_DIM)

    loads = [
        pltpu.make_async_copy(s, d, load_sem.at[i])
        for i, (s, d) in enumerate(
            ((k_hbm, k_buf), (v_hbm, v_buf), (wo_hbm, wo_buf), (wg_hbm.at[0], wg_buf), (wu_hbm.at[0], wu_buf), (wd_hbm.at[0], wd_buf))
        )
    ]
    for load in loads:
        load.start()

    barrier = pltpu.get_barrier_semaphore()

    def greet(k, _):
        pl.semaphore_signal(barrier, inc=1, device_id={"blk": rem(me + k, n)}, device_id_type=MESH)
        return 0

    lax.fori_loop(1, n, greet, 0)

    def remote(src, dst, ss, rs, k):
        return pltpu.make_async_remote_copy(
            src_ref=src, dst_ref=dst, send_sem=ss.at[k], recv_sem=rs.at[k],
            device_id={"blk": rem(me + k, n)}, device_id_type=MESH,
        )

    def spread(make):
        def step(k, _):
            make(k).start()
            return 0

        lax.fori_loop(1, n, step, 0)

    def arrive(make):
        def step(k, _):
            make(k).wait_recv()
            return 0

        lax.fori_loop(1, n, step, 0)

    def left(make):
        def step(k, _):
            make(k).wait_send()
            return 0

        lax.fori_loop(1, n, step, 0)

    for h in range(heads):
        q_tmp[h * rows : (h + 1) * rows, :] = q_ref[:, h * HEAD_DIM : (h + 1) * HEAD_DIM].astype(F32)
    q_all[me] = q_tmp[...].astype(BF16)
    pl.semaphore_wait(barrier, n - 1)
    send_q = lambda k: remote(q_all.at[me], q_all.at[me], q_ss, q_rs, k)
    spread(send_q)

    for c in range(parts):
        t_tmp[c * rows : (c + 1) * rows, :] = res_ref[:, c * cols : (c + 1) * cols].astype(F32)
    spread_rows = lambda o: div(o, TILE) * rows + rem(o, rows)
    repeat = select(n * TILE, total, spread_rows)
    part_of = div(rem(lax.broadcasted_iota(jnp.int32, (n * TILE, 1), 0), TILE), rows)
    named = jnp.where(ids_ref[...] == me, gates_ref[...], 0)
    high = jnp.sum(dot(repeat, lax.shift_right_logical(named, 8).astype(F32).astype(BF16)), axis=1, keepdims=True)
    low = jnp.sum(dot(repeat, lax.bitwise_and(named, 255).astype(F32).astype(BF16)), axis=1, keepdims=True)
    row_weight = (high * 256.0 + low) / 65536.0
    span = GROUP * total
    q_order = select(span, span, lambda o: div(rem(o, total), rows) * (GROUP * rows) + div(o, total) * rows + rem(o, rows))

    arrive(send_q)
    loads[0].wait()
    loads[1].wait()

    send_o = lambda k: remote(o_send.at[rem(me + k, n)], o_got.at[me], o_ss, o_rs, k)
    send_s = lambda k: remote(s_send.at[rem(me + k, n)], s_got.at[me], s_ss, s_rs, k)

    def attend(i, _):
        g = rem(div(me, per_kv) + (kv - 1 - i), kv)
        at = pl.ds(pl.multiple_of(g * HEAD_DIM, HEAD_DIM), HEAD_DIM)
        block = q_all[:, pl.ds(pl.multiple_of(g * (GROUP * rows), GROUP * rows), GROUP * rows), :]
        q = dot(q_order, block.reshape(span, HEAD_DIM)).astype(BF16)
        s = dot(k_buf[:, at], q, 1, 1)
        top = jnp.max(s, axis=0, keepdims=True)
        p = jnp.exp2((s - top) * scale)
        mass = jnp.sum(p, axis=0, keepdims=True)
        o = dot(v_buf[:, at], p.astype(BF16), 0, 0)
        lanes = own_heads * total
        for j in range(per_kv):
            t = g * per_kv + j
            o_send[t] = o[:, j * lanes : (j + 1) * lanes].astype(BF16)
            s_send[t, 0:1, :] = top[:, j * lanes : (j + 1) * lanes]
            s_send[t, 1:2, :] = mass[:, j * lanes : (j + 1) * lanes]
        for j in range(per_kv):
            t = g * per_kv + j

            @pl.when(t != me)
            def _():
                k = rem(t - me + n, n)
                send_s(k).start()
                send_o(k).start()

        return 0

    lax.fori_loop(0, kv, attend, 0)
    o_got[me] = o_send[me]
    s_got[me] = s_send[me]
    arrive(send_s)
    arrive(send_o)

    tops, masses = s_got[:, 0:1, :], s_got[:, 1:2, :]
    factor = jnp.exp2((tops - jnp.max(tops, axis=0, keepdims=True)) * scale)
    mass = jnp.sum(masses * factor, axis=0)
    out = o_got[0].astype(F32) * factor[0]
    for d in range(1, n):
        out = out + o_got[d].astype(F32) * factor[d]
    attended = (out / mass).astype(BF16)

    halves = [
        dot(select(n * TILE, own_heads * total, lambda o, j=j: j * total + spread_rows(o)), attended, 1, 1)
        for j in range(own_heads)
    ]
    lhs = jnp.concatenate(halves, axis=1)
    loads[2].wait()
    proj = None
    for c in range(parts):
        term = dot(jnp.where(part_of == c, lhs, 0.0).astype(BF16), wo_buf[:, c * cols : (c + 1) * cols])
        proj = term if proj is None else proj + term
    p_send[...] = proj.astype(BF16).reshape(n, TILE, cols)
    send_p = lambda k: remote(p_send.at[rem(me + k, n)], p_got.at[me], p_ss, p_rs, k)
    spread(send_p)
    p_got[me] = p_send[me]
    arrive(send_p)
    stream = t_tmp[...]
    for d in range(n):
        stream = stream + p_got[d].astype(F32)
    t_tmp[...] = stream
    squares = jnp.broadcast_to(jnp.sum(stream * stream, axis=1, keepdims=True), (TILE, 128))
    s_tmp[...] = squares
    whole = s_tmp[0:rows, :]
    for c in range(1, parts):
        whole = whole + s_tmp[c * rows : (c + 1) * rows, :]
    inverse = lax.rsqrt(whole[:, 0:1] / model + 1e-06)
    for c in range(parts):
        piece = t_tmp[c * rows : (c + 1) * rows, :]
        hid_ref[:, c * cols : (c + 1) * cols] = piece.astype(BF16)
        t_tmp[c * rows : (c + 1) * rows, :] = piece * inverse * gain_ref[:, c * cols : (c + 1) * cols]
    n_all[me] = t_tmp[...].astype(BF16)
    send_n = lambda k: remote(n_all.at[me], n_all.at[me], n_ss, n_rs, k)
    spread(send_n)
    by_part = select(n * TILE, n * TILE, lambda o: div(rem(o, total), rows) * TILE + div(o, total) * rows + rem(o, rows))
    for load in loads[3:]:
        load.wait()
    arrive(send_n)

    x = dot(by_part, n_all[...].reshape(n * TILE, cols)).astype(BF16)
    gate = up = None
    for c in range(parts):
        piece = x[c * total : (c + 1) * total, :]
        a, b = dot(piece, wg_buf[c * cols : (c + 1) * cols, :]), dot(piece, wu_buf[c * cols : (c + 1) * cols, :])
        gate, up = (a, b) if gate is None else (gate + a, up + b)
    inner = (gate / (1.0 + jnp.exp(-gate)) * up).astype(BF16)
    lhs = dot(repeat, inner)
    y = None
    for c in range(parts):
        term = dot(jnp.where(part_of == c, lhs, 0.0).astype(BF16), wd_buf[:, c * cols : (c + 1) * cols])
        y = term if y is None else y + term
    y_send[...] = (y * row_weight).astype(BF16).reshape(n, TILE, cols)
    send_y = lambda k: remote(y_send.at[rem(me + k, n)], y_got.at[me], y_ss, y_rs, k)
    spread(send_y)
    y_got[me] = y_send[me]
    for make in (send_q, send_s, send_o, send_p, send_n):
        left(make)
    arrive(send_y)
    moe = y_got[0].astype(F32)
    for d in range(1, n):
        moe = moe + y_got[d].astype(F32)
    t_tmp[...] = moe
    for c in range(parts):
        moe_ref[:, c * cols : (c + 1) * cols] = t_tmp[c * rows : (c + 1) * rows, :].astype(BF16)
    left(send_y)


def fused(n, queries, k_cache, v_cache, w_out, residual, gain, ids, gates, w_gate, w_up, w_down):
    rows, width = queries.shape
    model = residual.shape[1]
    heads = width // HEAD_DIM
    cols = model * rows // TILE
    lanes = heads // n * n * rows
    vmem, hbm = pl.BlockSpec(memory_space=pltpu.VMEM), pl.BlockSpec(memory_space=pl.ANY)
    block = lambda *shape, kind=BF16: pltpu.VMEM(shape, kind)
    message = block(n, TILE, cols)
    return pl.pallas_call(
        functools.partial(fused_kernel, n),
        out_shape=(jax.ShapeDtypeStruct(residual.shape, BF16),) * 2,
        in_specs=[vmem] * 5 + [hbm] * 6,
        out_specs=(vmem, vmem),
        scratch_shapes=[
            block(*k_cache.shape), block(*v_cache.shape), block(*w_out.shape),
            block(*w_gate.shape[1:]), block(*w_up.shape[1:]), block(*w_down.shape[1:]),
            block(heads * rows, HEAD_DIM, kind=F32), block(TILE, cols, kind=F32), block(TILE, 128, kind=F32),
            block(n, heads * rows, HEAD_DIM),
            block(n, HEAD_DIM, lanes), block(n, HEAD_DIM, lanes),
            block(n, 8, lanes, kind=F32), block(n, 8, lanes, kind=F32),
            message, message, message, message, message,
            pltpu.SemaphoreType.DMA((6,)),
        ] + [pltpu.SemaphoreType.DMA((n,))] * 12,
        compiler_params=pltpu.CompilerParams(
            collective_id=0, has_side_effects=True, vmem_limit_bytes=48 * 2**20
        ),
    )(queries, residual, gain.reshape(1, model), ids, gates, k_cache, v_cache, w_out, w_gate, w_up, w_down)


def solution(mesh):
    n = mesh.shape["blk"]

    def body(*blocks):
        if fits_fused(n, *blocks):
            return fused(n, *blocks)
        return shards(*blocks)

    return jax.shard_map(
        body,
        mesh=mesh,
        in_specs=(
            P(("groups", "blk"), None),
            P(("groups", "blk"), None),
            P(("groups", "blk"), None),
            P("blk", None),
            P(("groups", "blk"), None),
            P(),
            P("groups", None),
            P("groups", None),
            P("blk", None, None),
            P("blk", None, None),
            P("blk", None, None),
        ),
        out_specs=(P(("groups", "blk"), None), P(("groups", "blk"), None)),
        check_vma=False,
    )
```

```python
import functools
import math

import jax
import jax.numpy as jnp
from jax import lax
from jax.experimental import pallas as pl
from jax.experimental.pallas import tpu as pltpu
from jax.sharding import PartitionSpec as P

HEADS = 32
KV_HEADS = 4
HEAD_DIM = 128
GROUP = 8
CAPACITY = 64


def local_attend(query_rows, k_cache, v_cache):
    row_count = query_rows.shape[0]
    span = k_cache.shape[0]
    query_four = query_rows.reshape(row_count, KV_HEADS, GROUP, HEAD_DIM)
    key_three = k_cache.reshape(span, KV_HEADS, HEAD_DIM)
    value_three = v_cache.reshape(span, KV_HEADS, HEAD_DIM)
    scores = jnp.einsum(
        "rhgd,chd->rhgc", query_four, key_three, preferred_element_type=jnp.float32
    ) / jnp.sqrt(jnp.float32(HEAD_DIM))
    block_max = jnp.max(scores, axis=-1)
    probs = jnp.exp(scores - block_max[..., None])
    block_sum = jnp.sum(probs, axis=-1)
    block_out = jnp.einsum(
        "rhgc,chd->rhgd",
        probs.astype(jnp.bfloat16),
        value_three,
        preferred_element_type=jnp.float32,
    )
    return (
        block_out.reshape(row_count, HEADS * HEAD_DIM),
        block_max.reshape(row_count, HEADS),
        block_sum.reshape(row_count, HEADS),
    )


def shards(
    queries,
    k_cache,
    v_cache,
    w_out,
    residual,
    norm_gain,
    expert_ids,
    gate_fixed,
    w_gate,
    w_up,
    w_down,
):
    row_count = queries.shape[0]
    width_q = HEADS * HEAD_DIM
    devices = lax.axis_size("blk")
    every_query = lax.all_gather(queries, "blk", axis=0, tiled=True)
    total_rows = every_query.shape[0]
    block_rows = 128 if total_rows % 128 == 0 else total_rows
    stacked = every_query.reshape(total_rows // block_rows, block_rows, width_q)
    part_out, part_max, part_sum = lax.map(
        lambda piece: local_attend(piece, k_cache, v_cache), stacked
    )
    part_out = part_out.reshape(total_rows, width_q)
    part_max = part_max.reshape(total_rows, HEADS)
    part_sum = part_sum.reshape(total_rows, HEADS)
    got_out, got_max, got_sum = (
        lax.all_to_all(part_out, "blk", split_axis=0, concat_axis=0, tiled=True),
        lax.all_to_all(part_max, "blk", split_axis=0, concat_axis=0, tiled=True),
        lax.all_to_all(part_sum, "blk", split_axis=0, concat_axis=0, tiled=True),
    )
    got_out = got_out.reshape(devices, row_count, HEADS, HEAD_DIM)
    got_max = got_max.reshape(devices, row_count, HEADS)
    got_sum = got_sum.reshape(devices, row_count, HEADS)
    top = jnp.max(got_max, axis=0)
    factor = jnp.exp(got_max - top[None])
    sum_acc = jnp.sum(got_sum * factor, axis=0)
    out_acc = jnp.sum(got_out * factor[..., None], axis=0).reshape(row_count, width_q)
    attended = (
        (out_acc.reshape(row_count, HEADS, HEAD_DIM) / sum_acc[..., None])
        .reshape(row_count, width_q)
        .astype(jnp.bfloat16)
    )
    columns = lax.all_to_all(attended, "blk", split_axis=1, concat_axis=0, tiled=True)
    piece = columns
    proj = lax.psum_scatter(
        jnp.dot(piece, w_out, preferred_element_type=jnp.float32),
        "blk",
        scatter_dimension=0,
        tiled=True,
    )
    stream = residual.astype(jnp.float32) + proj
    hidden = stream.astype(jnp.bfloat16)
    normed = (
        stream * lax.rsqrt(jnp.mean(stream * stream, axis=-1, keepdims=True) + 1e-06) * norm_gain
    ).astype(jnp.bfloat16)
    every_row = lax.all_gather(normed, "blk", axis=0, tiled=True)
    expert = lax.axis_index("blk")
    named = expert_ids == expert
    taken = jnp.any(named, axis=1)
    row_weight = jnp.sum(jnp.where(named, gate_fixed.astype(jnp.float32) / 65536.0, 0.0), axis=1)
    order = jnp.arange(taken.shape[0], dtype=jnp.int32)
    upto = jnp.logical_and(order[None, :] <= order[:, None], taken[None, :])
    slot_of = jnp.sum(upto.astype(jnp.int32), axis=1) - 1
    slot_ids = jnp.arange(CAPACITY, dtype=jnp.int32)
    select = jnp.logical_and(slot_of[None, :] == slot_ids[:, None], taken[None, :])
    picked = jnp.dot(
        select.astype(jnp.bfloat16), every_row, preferred_element_type=jnp.float32
    ).astype(jnp.bfloat16)
    slot_weight = jnp.dot(select.astype(jnp.float32), row_weight, precision=lax.Precision.HIGHEST)
    gate_part = jnp.dot(picked, w_gate[0], preferred_element_type=jnp.float32)
    up_part = jnp.dot(picked, w_up[0], preferred_element_type=jnp.float32)
    inner = (jax.nn.silu(gate_part) * up_part).astype(jnp.bfloat16)
    result = jnp.dot(inner, w_down[0], preferred_element_type=jnp.float32) * slot_weight[:, None]
    select_back = select.astype(jnp.float32).T
    piece = select_back
    moe_total = lax.psum_scatter(
        jnp.dot(piece, result, precision=lax.Precision.HIGHEST),
        "blk",
        scatter_dimension=0,
        tiled=True,
    )
    return (hidden, moe_total.astype(jnp.bfloat16))


MESH = pl.DeviceIdType.MESH
TILE = 16
F32, BF16 = jnp.float32, jnp.bfloat16


def fits_fused(n, queries, k_cache, v_cache, w_out, residual, gain, ids, gates, w_gate, w_up, w_down):
    rows, width = queries.shape
    heads = width // HEAD_DIM
    return (
        n % 4 == 0
        and heads % n == 0
        and (heads // GROUP) % 2 == 0
        and (GROUP * n // heads) % 2 == 0
        and w_out.shape[0] % HEAD_DIM == 0
        and GROUP % (heads // n) == 0
        and (heads // n) * n * rows == HEAD_DIM
        and w_gate.shape[0] == 1
        and TILE % rows == 0
        and n * TILE == 256
        and residual.shape[1] % (TILE // rows * 128) == 0
    )


def select(out_rows, in_rows, source):
    o = lax.broadcasted_iota(jnp.int32, (out_rows, in_rows), 0)
    i = lax.broadcasted_iota(jnp.int32, (out_rows, in_rows), 1)
    return jnp.where(i == source(o), 1.0, 0.0).astype(BF16)


def dot(a, b, ca=1, cb=0):
    return lax.dot_general(a, b, (((ca,), (cb,)), ((), ())), preferred_element_type=F32)


def fused_kernel(
    n, q_hbm, res_hbm, gain_hbm, ids_hbm, gates_hbm, k_hbm, v_hbm, wo_hbm, wg_hbm, wu_hbm, wd_hbm,
    hid_ref, moe_ref,
    q_ref, res_ref, gain_ref, ids_ref, gates_ref,
    k_buf, v_buf, wo_buf, wg_buf, wu_buf, wd_buf, q_tmp, t_tmp, s_tmp,
    q_send, q_all, q_perm, o_send, o_got, s_send, s_got, p_send, p_got, n_all, y_send, y_got,
    load_sem, q_ss, q_rs, o_ss, o_rs, s_ss, s_rs, p_ss, p_rs, n_ss, n_rs, y_ss, y_rs,
    kv_ss, kv_rs, f_ss, f_rs,
):
    me = lax.axis_index("blk")
    rows, width = q_ref.shape
    model = res_ref.shape[1]
    heads = width // HEAD_DIM
    kv = heads // GROUP
    own_heads = heads // n
    half = n // 2
    core, pair = lax.rem(me, 2), lax.div(me, 2)
    mate = me + 1 - 2 * core
    mine = heads // 2 * rows
    total = n * rows
    parts = TILE // rows
    cols = model // parts
    div, rem = lax.div, lax.rem
    scale = math.log2(math.e) / math.sqrt(HEAD_DIM)

    kv_cols = k_buf.shape[2]
    kv_at = lambda which: pl.ds(pl.multiple_of(which * kv_cols, 128), kv_cols)
    moves = (
        (q_hbm, q_ref), (res_hbm, res_ref), (gain_hbm, gain_ref), (ids_hbm, ids_ref), (gates_hbm, gates_ref),
        (k_hbm.at[:, kv_at(core)], k_buf.at[core]), (v_hbm.at[:, kv_at(core)], v_buf.at[core]),
        (wo_hbm, wo_buf), (wg_hbm.at[0], wg_buf), (wu_hbm.at[0], wu_buf), (wd_hbm.at[0], wd_buf),
    )
    loads = [pltpu.make_async_copy(s, d, load_sem.at[i]) for i, (s, d) in enumerate(moves)]
    for load in loads:
        load.start()

    barrier = pltpu.get_barrier_semaphore()

    def greet(k, _):
        pl.semaphore_signal(barrier, inc=1, device_id={"blk": rem(me + k, n)}, device_id_type=MESH)
        return 0

    lax.fori_loop(1, n, greet, 0)

    def remote(src, dst, ss, rs, k):
        return pltpu.make_async_remote_copy(
            src_ref=src, dst_ref=dst, send_sem=ss.at[k], recv_sem=rs.at[k],
            device_id={"blk": rem(me + k, n)}, device_id_type=MESH,
        )

    def spread(make):
        def step(k, _):
            make(k).start()
            return 0

        lax.fori_loop(1, n, step, 0)

    def arrive(make):
        def step(k, _):
            make(k).wait_recv()
            return 0

        lax.fori_loop(1, n, step, 0)

    def left(make):
        def step(k, _):
            make(k).wait_send()
            return 0

        lax.fori_loop(1, n, step, 0)

    def move(src, dst, ss, rs, peer):
        return pltpu.make_async_remote_copy(
            src_ref=src, dst_ref=dst, send_sem=ss, recv_sem=rs, device_id={"blk": peer}, device_id_type=MESH
        )

    loads[0].wait()
    for h in range(heads):
        q_tmp[h * rows : (h + 1) * rows, :] = q_ref[:, h * HEAD_DIM : (h + 1) * HEAD_DIM].astype(F32)
    for c in range(2):
        q_send[c] = q_tmp[c * mine : (c + 1) * mine, :].astype(BF16)
    q_all[me] = q_send[core]
    pl.semaphore_wait(barrier, n - 1)
    send_q = lambda k: remote(q_send.at[rem(rem(me + k, n), 2)], q_all.at[me], q_ss, q_rs, k)
    spread(send_q)
    swaps = [
        move(src.at[:, kv_at(1 - core)], dst.at[core], kv_ss.at[i], kv_rs.at[i], mate)
        for i, (src, dst) in enumerate(((k_hbm, k_buf), (v_hbm, v_buf)))
    ]
    for swap in swaps:
        swap.start()
    for load in loads[1:5]:
        load.wait()

    for c in range(parts):
        t_tmp[c * rows : (c + 1) * rows, :] = res_ref[:, c * cols : (c + 1) * cols].astype(F32)
    spread_rows = lambda o: div(o, TILE) * rows + rem(o, rows)
    repeat = select(n * TILE, total, spread_rows)
    part_of = div(rem(lax.broadcasted_iota(jnp.int32, (n * TILE, 1), 0), TILE), rows)
    named = jnp.where(ids_ref[...] == me, gates_ref[...], 0)
    high = jnp.sum(dot(repeat, lax.shift_right_logical(named, 8).astype(F32).astype(BF16), 1, 1), axis=1, keepdims=True)
    low = jnp.sum(dot(repeat, lax.bitwise_and(named, 255).astype(F32).astype(BF16), 1, 1), axis=1, keepdims=True)
    row_weight = (high * 256.0 + low) / 65536.0
    span = GROUP * total
    q_order = select(span, span, lambda o: div(rem(o, total), rows) * (GROUP * rows) + div(o, total) * rows + rem(o, rows))

    arrive(send_q)
    lanes = own_heads * total
    for g in range(kv // 2):
        block = q_all[:, g * GROUP * rows : (g + 1) * GROUP * rows, :].reshape(span, HEAD_DIM)
        ordered = dot(q_order, block).astype(BF16)
        for u in range(span // (2 * lanes)):
            q_perm[g * (span // (2 * lanes)) + u] = ordered[u * 2 * lanes : (u + 1) * 2 * lanes]
    for load in loads[5:7]:
        load.wait()
    for swap in swaps:
        swap.wait_recv()

    def send_o(t):
        return move(o_send.at[t], o_got.at[pair], o_ss.at[t], o_rs.at[pair], core * half + t)

    def send_s(t):
        return move(s_send.at[t], s_got.at[pair], s_ss.at[t], s_rs.at[pair], core * half + t)

    steps = half // 2
    per_step = steps // (kv // 2)

    def attend(i, _):
        u = rem(div(pair, 2) + i, steps)
        at = pl.ds(pl.multiple_of(div(u, per_step) * HEAD_DIM, HEAD_DIM), HEAD_DIM)
        keys = k_buf[:, :, at].reshape(2 * k_buf.shape[1], HEAD_DIM)
        values = v_buf[:, :, at].reshape(2 * v_buf.shape[1], HEAD_DIM)
        s = dot(keys, q_perm[u], 1, 1)
        top = jnp.max(s, axis=0, keepdims=True)
        p = jnp.exp2((s - top) * scale)
        mass = jnp.sum(p, axis=0, keepdims=True)
        o = dot(values, p.astype(BF16), 0, 0)
        for j in range(2):
            t = 2 * u + j
            o_send[t] = o[:, j * lanes : (j + 1) * lanes].astype(BF16)
            s_send[t, 0:1, :] = top[:, j * lanes : (j + 1) * lanes]
            s_send[t, 1:2, :] = mass[:, j * lanes : (j + 1) * lanes]
        for j in range(2):
            t = 2 * u + j

            @pl.when(core * half + t != me)
            def _():
                send_s(t).start()
                send_o(t).start()

        return 0

    lax.fori_loop(0, steps, attend, 0)
    source_core = div(me, half)

    @pl.when(source_core == core)
    def _():
        o_got[pair] = o_send[me - core * half]
        s_got[pair] = s_send[me - core * half]

    def got(s, _):
        source = 2 * s + source_core

        @pl.when(source != me)
        def _():
            move(s_send.at[0], s_got.at[s], s_ss.at[0], s_rs.at[s], source).wait_recv()
            move(o_send.at[0], o_got.at[s], o_ss.at[0], o_rs.at[s], source).wait_recv()

        return 0

    lax.fori_loop(0, half, got, 0)

    tops, masses = s_got[:, 0:1, :], s_got[:, 1:2, :]
    factor = jnp.exp2((tops - jnp.max(tops, axis=0, keepdims=True)) * scale)
    mass = jnp.sum(masses * factor, axis=0)
    out = o_got[0].astype(F32) * factor[0]
    for d in range(1, half):
        out = out + o_got[d].astype(F32) * factor[d]
    attended = (out / mass).astype(BF16)

    halves = [
        dot(select(n * TILE, own_heads * total, lambda o, j=j: j * total + spread_rows(o)), attended, 1, 1)
        for j in range(own_heads)
    ]
    lhs = jnp.concatenate(halves, axis=1)
    loads[7].wait()
    proj = None
    for c in range(parts):
        term = dot(jnp.where(part_of == c, lhs, 0.0).astype(BF16), wo_buf[:, c * cols : (c + 1) * cols])
        proj = term if proj is None else proj + term
    p_send[...] = proj.astype(BF16).reshape(n, TILE, cols)
    send_p = lambda k: remote(p_send.at[rem(me + k, n)], p_got.at[me], p_ss, p_rs, k)
    spread(send_p)
    p_got[me] = p_send[me]
    arrive(send_p)
    stream = t_tmp[...]
    for d in range(n):
        stream = stream + p_got[d].astype(F32)
    t_tmp[...] = stream
    squares = jnp.broadcast_to(jnp.sum(stream * stream, axis=1, keepdims=True), (TILE, 128))
    s_tmp[...] = squares
    whole = s_tmp[0:rows, :]
    for c in range(1, parts):
        whole = whole + s_tmp[c * rows : (c + 1) * rows, :]
    inverse = lax.rsqrt(whole[:, 0:1] / model + 1e-06)
    for c in range(parts):
        piece = t_tmp[c * rows : (c + 1) * rows, :]
        hid_ref[:, c * cols : (c + 1) * cols] = piece.astype(BF16)
        t_tmp[c * rows : (c + 1) * rows, :] = piece * inverse * gain_ref[:, c * cols : (c + 1) * cols]
    n_all[me] = t_tmp[...].astype(BF16)
    def send_n(k):
        return move(n_all.at[me], n_all.at[me], n_ss.at[k], n_rs.at[k], rem(me + 2 * k, n))

    def got_n(k):
        block = n_all.at[rem(me - 2 * k + n, n)]
        return move(block, block, n_ss.at[k], n_rs.at[k], rem(me - 2 * k + n, n))

    def hand_on(k):
        block = n_all.at[rem(me - 2 * k + n, n)]
        return move(block, block, f_ss.at[k], f_rs.at[k], mate)

    def handed(k):
        block = n_all.at[rem(mate - 2 * k + n, n)]
        return move(block, block, f_ss.at[k], f_rs.at[k], mate)

    def each(first, make):
        def step(k, _):
            make(k)
            return 0

        lax.fori_loop(first, half, step, 0)

    each(1, lambda k: send_n(k).start())
    hand_on(0).start()
    by_part = select(n * TILE, n * TILE, lambda o: div(rem(o, total), rows) * TILE + div(o, total) * rows + rem(o, rows))
    for load in loads[8:]:
        load.wait()

    def relay(k):
        got_n(k).wait_recv()
        hand_on(k).start()

    each(1, relay)
    each(0, lambda k: handed(k).wait_recv())

    x = dot(by_part, n_all[...].reshape(n * TILE, cols)).astype(BF16)
    gate = up = None
    for c in range(parts):
        piece = x[c * total : (c + 1) * total, :]
        a, b = dot(piece, wg_buf[c * cols : (c + 1) * cols, :]), dot(piece, wu_buf[c * cols : (c + 1) * cols, :])
        gate, up = (a, b) if gate is None else (gate + a, up + b)
    inner = (gate / (1.0 + jnp.exp(-gate)) * up).astype(BF16)
    lhs = dot(repeat, inner)
    y = None
    for c in range(parts):
        term = dot(jnp.where(part_of == c, lhs, 0.0).astype(BF16), wd_buf[:, c * cols : (c + 1) * cols])
        y = term if y is None else y + term
    y_send[...] = (y * row_weight).astype(BF16).reshape(n, TILE, cols)
    send_y = lambda k: remote(y_send.at[rem(me + k, n)], y_got.at[me], y_ss, y_rs, k)
    spread(send_y)
    y_got[me] = y_send[me]
    left(send_q)
    for swap in swaps:
        swap.wait_send()

    def gone(t):
        @pl.when(core * half + t != me)
        def _():
            send_s(t).wait_send()
            send_o(t).wait_send()

    each(0, gone)
    left(send_p)
    each(1, lambda k: send_n(k).wait_send())
    each(0, lambda k: hand_on(k).wait_send())
    arrive(send_y)
    moe = y_got[0].astype(F32)
    for d in range(1, n):
        moe = moe + y_got[d].astype(F32)
    t_tmp[...] = moe
    for c in range(parts):
        moe_ref[:, c * cols : (c + 1) * cols] = t_tmp[c * rows : (c + 1) * rows, :].astype(BF16)
    left(send_y)


def fused(n, queries, k_cache, v_cache, w_out, residual, gain, ids, gates, w_gate, w_up, w_down):
    rows, width = queries.shape
    model = residual.shape[1]
    heads = width // HEAD_DIM
    cols = model * rows // TILE
    lanes = heads // n * n * rows
    vmem, hbm = pl.BlockSpec(memory_space=pltpu.VMEM), pl.BlockSpec(memory_space=pl.ANY)
    block = lambda *shape, kind=BF16: pltpu.VMEM(shape, kind)
    message = block(n, TILE, cols)
    return pl.pallas_call(
        functools.partial(fused_kernel, n),
        out_shape=(jax.ShapeDtypeStruct(residual.shape, BF16),) * 2,
        in_specs=[hbm] * 11,
        out_specs=(vmem, vmem),
        scratch_shapes=[
            block(rows, width), block(rows, model), block(1, model, kind=F32),
            block(*ids.shape[::-1], kind=jnp.int32), block(*gates.shape[::-1], kind=jnp.int32),
            block(2, k_cache.shape[0], k_cache.shape[1] // 2), block(2, v_cache.shape[0], v_cache.shape[1] // 2),
            block(*w_out.shape),
            block(*w_gate.shape[1:]), block(*w_up.shape[1:]), block(*w_down.shape[1:]),
            block(heads * rows, HEAD_DIM, kind=F32), block(TILE, cols, kind=F32), block(TILE, 128, kind=F32),
            block(2, heads // 2 * rows, HEAD_DIM), block(n, heads // 2 * rows, HEAD_DIM),
            block(n // 4, 2 * lanes, HEAD_DIM),
            block(n // 2, HEAD_DIM, lanes), block(n // 2, HEAD_DIM, lanes),
            block(n // 2, 8, lanes, kind=F32), block(n // 2, 8, lanes, kind=F32),
            message, message, message, message, message,
            pltpu.SemaphoreType.DMA((11,)),
        ] + [pltpu.SemaphoreType.DMA((n,))] * 12 + [pltpu.SemaphoreType.DMA((2,))] * 2
        + [pltpu.SemaphoreType.DMA((n // 2,))] * 2,
        compiler_params=pltpu.CompilerParams(
            collective_id=0, has_side_effects=True, vmem_limit_bytes=60 * 2**20
        ),
    )(queries, residual, gain.reshape(1, model), ids.T, gates.T, k_cache, v_cache, w_out, w_gate, w_up, w_down)


def solution(mesh):
    n = mesh.shape["blk"]

    def body(*blocks):
        if fits_fused(n, *blocks):
            return fused(n, *blocks)
        return shards(*blocks)

    return jax.shard_map(
        body,
        mesh=mesh,
        in_specs=(
            P(("groups", "blk"), None),
            P(("groups", "blk"), None),
            P(("groups", "blk"), None),
            P("blk", None),
            P(("groups", "blk"), None),
            P(),
            P("groups", None),
            P("groups", None),
            P("blk", None, None),
            P("blk", None, None),
            P("blk", None, None),
        ),
        out_specs=(P(("groups", "blk"), None), P(("groups", "blk"), None)),
        check_vma=False,
    )
```

```python
import functools
import math

import jax
import jax.numpy as jnp
from jax import lax
from jax.experimental import pallas as pl
from jax.experimental.pallas import tpu as pltpu
from jax.sharding import PartitionSpec as P

HEADS = 32
KV_HEADS = 4
HEAD_DIM = 128
GROUP = 8
CAPACITY = 64


def local_attend(query_rows, k_cache, v_cache):
    row_count = query_rows.shape[0]
    span = k_cache.shape[0]
    query_four = query_rows.reshape(row_count, KV_HEADS, GROUP, HEAD_DIM)
    key_three = k_cache.reshape(span, KV_HEADS, HEAD_DIM)
    value_three = v_cache.reshape(span, KV_HEADS, HEAD_DIM)
    scores = jnp.einsum(
        "rhgd,chd->rhgc", query_four, key_three, preferred_element_type=jnp.float32
    ) / jnp.sqrt(jnp.float32(HEAD_DIM))
    block_max = jnp.max(scores, axis=-1)
    probs = jnp.exp(scores - block_max[..., None])
    block_sum = jnp.sum(probs, axis=-1)
    block_out = jnp.einsum(
        "rhgc,chd->rhgd",
        probs.astype(jnp.bfloat16),
        value_three,
        preferred_element_type=jnp.float32,
    )
    return (
        block_out.reshape(row_count, HEADS * HEAD_DIM),
        block_max.reshape(row_count, HEADS),
        block_sum.reshape(row_count, HEADS),
    )


def shards(
    queries,
    k_cache,
    v_cache,
    w_out,
    residual,
    norm_gain,
    expert_ids,
    gate_fixed,
    w_gate,
    w_up,
    w_down,
):
    row_count = queries.shape[0]
    width_q = HEADS * HEAD_DIM
    devices = lax.axis_size("blk")
    every_query = lax.all_gather(queries, "blk", axis=0, tiled=True)
    total_rows = every_query.shape[0]
    block_rows = 128 if total_rows % 128 == 0 else total_rows
    stacked = every_query.reshape(total_rows // block_rows, block_rows, width_q)
    part_out, part_max, part_sum = lax.map(
        lambda piece: local_attend(piece, k_cache, v_cache), stacked
    )
    part_out = part_out.reshape(total_rows, width_q)
    part_max = part_max.reshape(total_rows, HEADS)
    part_sum = part_sum.reshape(total_rows, HEADS)
    got_out, got_max, got_sum = (
        lax.all_to_all(part_out, "blk", split_axis=0, concat_axis=0, tiled=True),
        lax.all_to_all(part_max, "blk", split_axis=0, concat_axis=0, tiled=True),
        lax.all_to_all(part_sum, "blk", split_axis=0, concat_axis=0, tiled=True),
    )
    got_out = got_out.reshape(devices, row_count, HEADS, HEAD_DIM)
    got_max = got_max.reshape(devices, row_count, HEADS)
    got_sum = got_sum.reshape(devices, row_count, HEADS)
    top = jnp.max(got_max, axis=0)
    factor = jnp.exp(got_max - top[None])
    sum_acc = jnp.sum(got_sum * factor, axis=0)
    out_acc = jnp.sum(got_out * factor[..., None], axis=0).reshape(row_count, width_q)
    attended = (
        (out_acc.reshape(row_count, HEADS, HEAD_DIM) / sum_acc[..., None])
        .reshape(row_count, width_q)
        .astype(jnp.bfloat16)
    )
    columns = lax.all_to_all(attended, "blk", split_axis=1, concat_axis=0, tiled=True)
    piece = columns
    proj = lax.psum_scatter(
        jnp.dot(piece, w_out, preferred_element_type=jnp.float32),
        "blk",
        scatter_dimension=0,
        tiled=True,
    )
    stream = residual.astype(jnp.float32) + proj
    hidden = stream.astype(jnp.bfloat16)
    normed = (
        stream * lax.rsqrt(jnp.mean(stream * stream, axis=-1, keepdims=True) + 1e-06) * norm_gain
    ).astype(jnp.bfloat16)
    every_row = lax.all_gather(normed, "blk", axis=0, tiled=True)
    expert = lax.axis_index("blk")
    named = expert_ids == expert
    taken = jnp.any(named, axis=1)
    row_weight = jnp.sum(jnp.where(named, gate_fixed.astype(jnp.float32) / 65536.0, 0.0), axis=1)
    order = jnp.arange(taken.shape[0], dtype=jnp.int32)
    upto = jnp.logical_and(order[None, :] <= order[:, None], taken[None, :])
    slot_of = jnp.sum(upto.astype(jnp.int32), axis=1) - 1
    slot_ids = jnp.arange(CAPACITY, dtype=jnp.int32)
    select = jnp.logical_and(slot_of[None, :] == slot_ids[:, None], taken[None, :])
    picked = jnp.dot(
        select.astype(jnp.bfloat16), every_row, preferred_element_type=jnp.float32
    ).astype(jnp.bfloat16)
    slot_weight = jnp.dot(select.astype(jnp.float32), row_weight, precision=lax.Precision.HIGHEST)
    gate_part = jnp.dot(picked, w_gate[0], preferred_element_type=jnp.float32)
    up_part = jnp.dot(picked, w_up[0], preferred_element_type=jnp.float32)
    inner = (jax.nn.silu(gate_part) * up_part).astype(jnp.bfloat16)
    result = jnp.dot(inner, w_down[0], preferred_element_type=jnp.float32) * slot_weight[:, None]
    select_back = select.astype(jnp.float32).T
    piece = select_back
    moe_total = lax.psum_scatter(
        jnp.dot(piece, result, precision=lax.Precision.HIGHEST),
        "blk",
        scatter_dimension=0,
        tiled=True,
    )
    return (hidden, moe_total.astype(jnp.bfloat16))


MESH = pl.DeviceIdType.MESH
TILE = 16
F32, BF16 = jnp.float32, jnp.bfloat16


def fits_fused(n, queries, k_cache, v_cache, w_out, residual, gain, ids, gates, w_gate, w_up, w_down):
    rows, width = queries.shape
    heads = width // HEAD_DIM
    return (
        n % 4 == 0
        and heads % n == 0
        and (heads // GROUP) % 2 == 0
        and (GROUP * n // heads) % 2 == 0
        and w_out.shape[0] % HEAD_DIM == 0
        and GROUP % (heads // n) == 0
        and (heads // n) * n * rows == HEAD_DIM
        and w_gate.shape[0] == 1
        and TILE % rows == 0
        and n * TILE == 256
        and residual.shape[1] % (TILE // rows * 128) == 0
    )


def select(out_rows, in_rows, source):
    o = lax.broadcasted_iota(jnp.int32, (out_rows, in_rows), 0)
    i = lax.broadcasted_iota(jnp.int32, (out_rows, in_rows), 1)
    return jnp.where(i == source(o), 1.0, 0.0).astype(BF16)


def dot(a, b, ca=1, cb=0):
    return lax.dot_general(a, b, (((ca,), (cb,)), ((), ())), preferred_element_type=F32)


def fused_kernel(
    n, q_hbm, res_hbm, gain_hbm, ids_hbm, gates_hbm, k_hbm, v_hbm, wo_hbm, wg_hbm, wu_hbm, wd_hbm,
    hid_ref, moe_ref,
    q_ref, res_ref, gain_ref, ids_ref, gates_ref,
    k_buf, v_buf, wo_buf, wg_buf, wu_buf, wd_buf, q_tmp, t_tmp, s_tmp,
    q_send, q_all, q_perm, f_loc, o_send, o_got, s_send, s_got, p_send, p_met, p_sum, p_got, n_all, y_send, y_met, y_sum, y_got,
    load_sem, q_ss, q_rs, o_ss, o_rs, s_ss, s_rs, p_ss, p_rs, n_ss, n_rs, y_ss, y_rs,
    kv_ss, kv_rs, f_ss, f_rs,
):
    me = lax.axis_index("blk")
    rows, width = q_ref.shape
    model = res_ref.shape[1]
    heads = width // HEAD_DIM
    kv = heads // GROUP
    own_heads = heads // n
    half = n // 2
    core, pair = lax.rem(me, 2), lax.div(me, 2)
    mate = me + 1 - 2 * core
    mine = heads // 2 * rows
    total = n * rows
    parts = TILE // rows
    cols = model // parts
    div, rem = lax.div, lax.rem
    scale = math.log2(math.e) / math.sqrt(HEAD_DIM)

    kv_cols = k_buf.shape[2]
    kv_at = lambda which: pl.ds(pl.multiple_of(which * kv_cols, 128), kv_cols)
    moves = (
        (q_hbm, q_ref), (res_hbm, res_ref), (gain_hbm, gain_ref), (ids_hbm, ids_ref), (gates_hbm, gates_ref),
        (k_hbm.at[:, kv_at(core)], k_buf.at[core]), (v_hbm.at[:, kv_at(core)], v_buf.at[core]),
        (wo_hbm, wo_buf), (wg_hbm.at[0], wg_buf), (wu_hbm.at[0], wu_buf), (wd_hbm.at[0], wd_buf),
    )
    loads = [pltpu.make_async_copy(s, d, load_sem.at[i]) for i, (s, d) in enumerate(moves)]
    for load in loads:
        load.start()

    barrier = pltpu.get_barrier_semaphore()

    def greet(k, _):
        pl.semaphore_signal(barrier, inc=1, device_id={"blk": rem(me + k, n)}, device_id_type=MESH)
        return 0

    lax.fori_loop(1, n, greet, 0)

    def remote(src, dst, ss, rs, k):
        return pltpu.make_async_remote_copy(
            src_ref=src, dst_ref=dst, send_sem=ss.at[k], recv_sem=rs.at[k],
            device_id={"blk": rem(me + k, n)}, device_id_type=MESH,
        )

    def spread(make):
        def step(k, _):
            make(k).start()
            return 0

        lax.fori_loop(1, n, step, 0)

    def arrive(make):
        def step(k, _):
            make(k).wait_recv()
            return 0

        lax.fori_loop(1, n, step, 0)

    def left(make):
        def step(k, _):
            make(k).wait_send()
            return 0

        lax.fori_loop(1, n, step, 0)

    def move(src, dst, ss, rs, peer):
        return pltpu.make_async_remote_copy(
            src_ref=src, dst_ref=dst, send_sem=ss, recv_sem=rs, device_id={"blk": peer}, device_id_type=MESH
        )

    loads[0].wait()
    for h in range(heads):
        q_tmp[h * rows : (h + 1) * rows, :] = q_ref[:, h * HEAD_DIM : (h + 1) * HEAD_DIM].astype(F32)
    for c in range(2):
        q_send[c] = q_tmp[c * mine : (c + 1) * mine, :].astype(BF16)
    q_all[me] = q_send[core]
    pl.semaphore_wait(barrier, n - 1)
    send_q = lambda k: remote(q_send.at[rem(rem(me + k, n), 2)], q_all.at[me], q_ss, q_rs, k)
    spread(send_q)
    swaps = [
        move(src.at[:, kv_at(1 - core)], dst.at[core], kv_ss.at[i], kv_rs.at[i], mate)
        for i, (src, dst) in enumerate(((k_hbm, k_buf), (v_hbm, v_buf)))
    ]
    for swap in swaps:
        swap.start()
    for load in loads[1:5]:
        load.wait()

    for c in range(parts):
        t_tmp[c * rows : (c + 1) * rows, :] = res_ref[:, c * cols : (c + 1) * cols].astype(F32)
    owner = lambda o: 2 * rem(div(o, TILE), half) + div(o, TILE * half)
    spread_rows = lambda o: owner(o) * rows + rem(o, rows)
    repeat = select(n * TILE, total, spread_rows)
    part_of = div(rem(lax.broadcasted_iota(jnp.int32, (n * TILE, 1), 0), TILE), rows)
    named = jnp.where(ids_ref[...] == me, gates_ref[...], 0)
    high = jnp.sum(dot(repeat, lax.shift_right_logical(named, 8).astype(F32).astype(BF16), 1, 1), axis=1, keepdims=True)
    low = jnp.sum(dot(repeat, lax.bitwise_and(named, 255).astype(F32).astype(BF16), 1, 1), axis=1, keepdims=True)
    row_weight = (high * 256.0 + low) / 65536.0
    span = GROUP * total
    q_order = select(span, span, lambda o: div(rem(o, total), rows) * (GROUP * rows) + div(o, total) * rows + rem(o, rows))

    arrive(send_q)
    lanes = own_heads * total
    for g in range(kv // 2):
        block = q_all[:, g * GROUP * rows : (g + 1) * GROUP * rows, :].reshape(span, HEAD_DIM)
        ordered = dot(q_order, block).astype(BF16)
        for u in range(span // (2 * lanes)):
            q_perm[g * (span // (2 * lanes)) + u] = ordered[u * 2 * lanes : (u + 1) * 2 * lanes]
    for load in loads[5:7]:
        load.wait()
    for swap in swaps:
        swap.wait_recv()

    def send_o(t):
        return move(o_send.at[t], o_got.at[pair], o_ss.at[t], o_rs.at[pair], core * half + t)

    def send_s(t):
        return move(s_send.at[t], s_got.at[pair], s_ss.at[t], s_rs.at[pair], core * half + t)

    steps = half // 2
    per_step = steps // (kv // 2)

    def attend(i, _):
        u = rem(div(pair, 2) + i, steps)
        at = pl.ds(pl.multiple_of(div(u, per_step) * HEAD_DIM, HEAD_DIM), HEAD_DIM)
        keys = k_buf[:, :, at].reshape(2 * k_buf.shape[1], HEAD_DIM)
        values = v_buf[:, :, at].reshape(2 * v_buf.shape[1], HEAD_DIM)
        s = dot(keys, q_perm[u], 1, 1)
        top = jnp.max(s, axis=0, keepdims=True)
        p = jnp.exp2((s - top) * scale)
        mass = jnp.sum(p, axis=0, keepdims=True)
        o = dot(values, p.astype(BF16), 0, 0)
        for j in range(2):
            t = 2 * u + j
            o_send[t] = o[:, j * lanes : (j + 1) * lanes].astype(BF16)
            s_send[t, 0:1, :] = top[:, j * lanes : (j + 1) * lanes]
            s_send[t, 1:2, :] = mass[:, j * lanes : (j + 1) * lanes]
        for j in range(2):
            t = 2 * u + j

            @pl.when(core * half + t != me)
            def _():
                send_s(t).start()
                send_o(t).start()

        return 0

    lax.fori_loop(0, steps, attend, 0)
    source_core = div(me, half)

    @pl.when(source_core == core)
    def _():
        o_got[pair] = o_send[me - core * half]
        s_got[pair] = s_send[me - core * half]

    def got(s, _):
        source = 2 * s + source_core

        @pl.when(source != me)
        def _():
            move(s_send.at[0], s_got.at[s], s_ss.at[0], s_rs.at[s], source).wait_recv()
            move(o_send.at[0], o_got.at[s], o_ss.at[0], o_rs.at[s], source).wait_recv()

        return 0

    lax.fori_loop(0, half, got, 0)

    tops, masses = s_got[:, 0:1, :], s_got[:, 1:2, :]
    factor = jnp.exp2((tops - jnp.max(tops, axis=0, keepdims=True)) * scale)
    mass = jnp.sum(masses * factor, axis=0)
    out = o_got[0].astype(F32) * factor[0]
    for d in range(1, half):
        out = out + o_got[d].astype(F32) * factor[d]
    attended = (out / mass).astype(BF16)

    def across(ss, rs, out, met, sums, got):
        swap = move(out, met, ss.at[0], rs.at[0], mate)

        def ship(k):
            to = rem(pair + k, half)
            return move(sums.at[to], got.at[pair], ss.at[k], rs.at[k], 2 * to + core)

        return swap, ship

    def add_up(values, out, met, sums, got, swap, ship):
        f_loc[...] = values.reshape(n, TILE, cols)
        out[...] = f_loc[pl.ds((1 - core) * half, half)].astype(BF16)
        swap.start()
        swap.wait_recv()
        sums[...] = (f_loc[pl.ds(core * half, half)] + met[...].astype(F32)).astype(BF16)
        for k in range(1, half):
            ship(k).start()
        got[pair] = sums[pair]

    halves = [
        dot(select(n * TILE, own_heads * total, lambda o, j=j: j * total + spread_rows(o)), attended, 1, 1)
        for j in range(own_heads)
    ]
    lhs = jnp.concatenate(halves, axis=1)
    loads[7].wait()
    proj = None
    for c in range(parts):
        term = dot(jnp.where(part_of == c, lhs, 0.0).astype(BF16), wo_buf[:, c * cols : (c + 1) * cols])
        proj = term if proj is None else proj + term
    swap_p, ship_p = across(p_ss, p_rs, p_send, p_met, p_sum, p_got)
    add_up(proj, p_send, p_met, p_sum, p_got, swap_p, ship_p)
    for k in range(1, half):
        back = rem(pair - k + half, half)
        move(p_sum.at[0], p_got.at[back], p_ss.at[k], p_rs.at[k], 2 * back + core).wait_recv()
    stream = t_tmp[...]
    for d in range(half):
        stream = stream + p_got[d].astype(F32)
    t_tmp[...] = stream
    squares = jnp.broadcast_to(jnp.sum(stream * stream, axis=1, keepdims=True), (TILE, 128))
    s_tmp[...] = squares
    whole = s_tmp[0:rows, :]
    for c in range(1, parts):
        whole = whole + s_tmp[c * rows : (c + 1) * rows, :]
    inverse = lax.rsqrt(whole[:, 0:1] / model + 1e-06)
    for c in range(parts):
        piece = t_tmp[c * rows : (c + 1) * rows, :]
        hid_ref[:, c * cols : (c + 1) * cols] = piece.astype(BF16)
        t_tmp[c * rows : (c + 1) * rows, :] = piece * inverse * gain_ref[:, c * cols : (c + 1) * cols]
    n_all[me] = t_tmp[...].astype(BF16)
    def send_n(k):
        return move(n_all.at[me], n_all.at[me], n_ss.at[k], n_rs.at[k], rem(me + 2 * k, n))

    def got_n(k):
        block = n_all.at[rem(me - 2 * k + n, n)]
        return move(block, block, n_ss.at[k], n_rs.at[k], rem(me - 2 * k + n, n))

    def hand_on(k):
        block = n_all.at[rem(me - 2 * k + n, n)]
        return move(block, block, f_ss.at[k], f_rs.at[k], mate)

    def handed(k):
        block = n_all.at[rem(mate - 2 * k + n, n)]
        return move(block, block, f_ss.at[k], f_rs.at[k], mate)

    def each(first, make):
        def step(k, _):
            make(k)
            return 0

        lax.fori_loop(first, half, step, 0)

    each(1, lambda k: send_n(k).start())
    hand_on(0).start()
    by_part = select(n * TILE, n * TILE, lambda o: div(rem(o, total), rows) * TILE + div(o, total) * rows + rem(o, rows))
    for load in loads[8:]:
        load.wait()

    def relay(k):
        got_n(k).wait_recv()
        hand_on(k).start()

    each(1, relay)
    each(0, lambda k: handed(k).wait_recv())

    x = dot(by_part, n_all[...].reshape(n * TILE, cols)).astype(BF16)
    gate = up = None
    for c in range(parts):
        piece = x[c * total : (c + 1) * total, :]
        a, b = dot(piece, wg_buf[c * cols : (c + 1) * cols, :]), dot(piece, wu_buf[c * cols : (c + 1) * cols, :])
        gate, up = (a, b) if gate is None else (gate + a, up + b)
    inner = (gate / (1.0 + jnp.exp(-gate)) * up).astype(BF16)
    lhs = dot(repeat, inner)
    y = None
    for c in range(parts):
        term = dot(jnp.where(part_of == c, lhs, 0.0).astype(BF16), wd_buf[:, c * cols : (c + 1) * cols])
        y = term if y is None else y + term
    swap_y, ship_y = across(y_ss, y_rs, y_send, y_met, y_sum, y_got)
    add_up(y * row_weight, y_send, y_met, y_sum, y_got, swap_y, ship_y)
    left(send_q)
    for swap in swaps:
        swap.wait_send()

    def gone(t):
        @pl.when(core * half + t != me)
        def _():
            send_s(t).wait_send()
            send_o(t).wait_send()

    each(0, gone)
    swap_p.wait_send()
    each(1, lambda k: ship_p(k).wait_send())
    each(1, lambda k: send_n(k).wait_send())
    each(0, lambda k: hand_on(k).wait_send())
    for k in range(1, half):
        back = rem(pair - k + half, half)
        move(y_sum.at[0], y_got.at[back], y_ss.at[k], y_rs.at[k], 2 * back + core).wait_recv()
    moe = y_got[0].astype(F32)
    for d in range(1, half):
        moe = moe + y_got[d].astype(F32)
    t_tmp[...] = moe
    for c in range(parts):
        moe_ref[:, c * cols : (c + 1) * cols] = t_tmp[c * rows : (c + 1) * rows, :].astype(BF16)
    swap_y.wait_send()
    each(1, lambda k: ship_y(k).wait_send())


def fused(n, queries, k_cache, v_cache, w_out, residual, gain, ids, gates, w_gate, w_up, w_down):
    rows, width = queries.shape
    model = residual.shape[1]
    heads = width // HEAD_DIM
    cols = model * rows // TILE
    lanes = heads // n * n * rows
    vmem, hbm = pl.BlockSpec(memory_space=pltpu.VMEM), pl.BlockSpec(memory_space=pl.ANY)
    block = lambda *shape, kind=BF16: pltpu.VMEM(shape, kind)
    part = block(n // 2, TILE, cols)
    return pl.pallas_call(
        functools.partial(fused_kernel, n),
        out_shape=(jax.ShapeDtypeStruct(residual.shape, BF16),) * 2,
        in_specs=[hbm] * 11,
        out_specs=(vmem, vmem),
        scratch_shapes=[
            block(rows, width), block(rows, model), block(1, model, kind=F32),
            block(*ids.shape[::-1], kind=jnp.int32), block(*gates.shape[::-1], kind=jnp.int32),
            block(2, k_cache.shape[0], k_cache.shape[1] // 2), block(2, v_cache.shape[0], v_cache.shape[1] // 2),
            block(*w_out.shape),
            block(*w_gate.shape[1:]), block(*w_up.shape[1:]), block(*w_down.shape[1:]),
            block(heads * rows, HEAD_DIM, kind=F32), block(TILE, cols, kind=F32), block(TILE, 128, kind=F32),
            block(2, heads // 2 * rows, HEAD_DIM), block(n, heads // 2 * rows, HEAD_DIM),
            block(n // 4, 2 * lanes, HEAD_DIM), block(n, TILE, cols, kind=F32),
            block(n // 2, HEAD_DIM, lanes), block(n // 2, HEAD_DIM, lanes),
            block(n // 2, 8, lanes, kind=F32), block(n // 2, 8, lanes, kind=F32),
            *(part,) * 4, block(n, TILE, cols), *(part,) * 4,
            pltpu.SemaphoreType.DMA((11,)),
        ] + [pltpu.SemaphoreType.DMA((n,))] * 12 + [pltpu.SemaphoreType.DMA((2,))] * 2
        + [pltpu.SemaphoreType.DMA((n // 2,))] * 2,
        compiler_params=pltpu.CompilerParams(
            collective_id=0, has_side_effects=True, vmem_limit_bytes=60 * 2**20
        ),
    )(queries, residual, gain.reshape(1, model), ids.T, gates.T, k_cache, v_cache, w_out, w_gate, w_up, w_down)


def solution(mesh):
    n = mesh.shape["blk"]

    def body(*blocks):
        if fits_fused(n, *blocks):
            return fused(n, *blocks)
        return shards(*blocks)

    return jax.shard_map(
        body,
        mesh=mesh,
        in_specs=(
            P(("groups", "blk"), None),
            P(("groups", "blk"), None),
            P(("groups", "blk"), None),
            P("blk", None),
            P(("groups", "blk"), None),
            P(),
            P("groups", None),
            P("groups", None),
            P("blk", None, None),
            P("blk", None, None),
            P("blk", None, None),
        ),
        out_specs=(P(("groups", "blk"), None), P(("groups", "blk"), None)),
        check_vma=False,
    )
```
